128 devices in a mesh: row: 8 (over z_hi, y), col: 8 (over z_lo, x), slab: 2 (over core).
Axes of the slice: x: 4, y: 4, z: 4 (z_hi: 2, z_lo: 2; z = z_hi * 2 + z_lo), core: 2. Of those that a mesh axis runs over, the one named last changes fastest.
Arguments:
- amplitudes: bfloat16 [56, 32, 56, 400], P('col', None, 'row', 'slab'), may hold values from -6 to 6
- integrals: bfloat16 [56, 400, 56, 400], P('row', 'slab', 'col'), may hold values from -0.0390625 to 0.0390625
Outputs:
- residual: float32 [56, 32, 56, 400], P('row', None, 'col', 'slab')
The draws below stay inside these ranges and needn't reach their ends.
All inputs are finite; a program needn't handle non-finite values.
Results may differ from the reference program's by a relative error of at most 0.0003.
Values may be sent and summed in bfloat16 or wider, within the bound.
No kernel may reach another device: no remote copies, remote signals or barrier semaphores. Data moves between devices by JAX's collectives and lax.ppermute only.
A program may use at most 192 MiB of HBM per device.

```python
import jax
import jax.numpy as jnp
from jax import lax

OCC = 56
VIR = 400
ASLAB = 32


def strengthened(values, own_key, source, target, shards_of, factor):
    def block_of(position):
        return (jnp.arange(values.shape[position]) // (values.shape[position] // shards_of)).reshape((-1,) + (1,) * (values.ndim - 1 - position))

    first = jax.random.permutation(own_key, shards_of)[block_of(target)]
    second = (block_of(target) + shards_of // 2) % shards_of
    return jnp.where((block_of(source) == first) | (block_of(source) == second), factor * values, values)


def block_scale(own_key, dims, cuts, least, top_value):
    def one(axis_at, shards_of):
        heights = jax.random.uniform(jax.random.fold_in(jax.random.fold_in(own_key, 6), axis_at), (shards_of,), jnp.float32, least / len(cuts), top_value / len(cuts))
        return jnp.repeat(jnp.exp(heights), dims[axis_at] // shards_of).reshape((-1,) + (1,) * (len(dims) - axis_at - 1))

    loudness = one(*cuts[0])
    for cut in cuts[1:]:
        loudness = loudness * one(*cut)
    return loudness


def centred(own_key, extent, scale, reach, pieces=(), kind=jnp.bfloat16):
    loudness = block_scale(own_key, extent, pieces, -0.22, 0.18) if pieces else 1.0
    result = jax.random.normal(own_key, extent, jnp.float32) * scale * loudness
    return jnp.minimum(jnp.maximum(result, -reach), reach).astype(kind)


def noise_with(key, shape, width, bound, shards, heavy, kind=jnp.bfloat16):
    array = width * jax.random.normal(key, shape, jnp.float32)
    if shards:
        array = array * block_scale(key, shape, shards, -0.22, 0.18)
    return jnp.clip(strengthened(array, jax.random.fold_in(key, 3), *heavy), -bound, bound).astype(kind)


def setup_inputs(seed: int = 0) -> dict:
    keys = jax.random.split(jax.random.key(seed), 3)
    return {
        "amplitudes": noise_with(keys[0], (OCC, ASLAB, OCC, VIR), 1.0, 6.0, ((0, 8), (2, 8), (3, 2)), (2, 0, 8, 2.0)),
        "integrals": centred(keys[1], (OCC, VIR, OCC, VIR), (OCC * VIR) ** -0.5, 0.0390625, ((0, 8), (1, 2), (2, 8))),
    }


def reference(amplitudes, integrals):
    amp_matrix = amplitudes.reshape(OCC * ASLAB, OCC * VIR)

    def one_column(occ_index):
        column = lax.dynamic_index_in_dim(integrals, occ_index, 2, keepdims=False)
        product = jnp.dot(amp_matrix, column.reshape(OCC * VIR, VIR), preferred_element_type=jnp.float32)
        return product.reshape(OCC, ASLAB, VIR)

    stacked = lax.map(one_column, jnp.arange(OCC, dtype=jnp.int32))
    cycle_term = jnp.transpose(stacked, (1, 2, 0, 3))
    return cycle_term - jnp.transpose(cycle_term, (2, 1, 0, 3))
```

```python
import jax
import jax.numpy as jnp
from jax import lax
from jax.experimental import pallas as pl
from jax.experimental.pallas import tpu as pltpu
from jax.sharding import PartitionSpec as P

CHUNKS = (1, 2, 2, 2)
LANE = 128
GAIN = 2.0**7.875
VMEM = 60 * 1024 * 1024


def padded(size):
    return -(-size // LANE) * LANE


def whole():
    return pl.BlockSpec(memory_space=pltpu.VMEM)


def params():
    return pltpu.CompilerParams(vmem_limit_bytes=VMEM)


def encode(values, used):
    top = jnp.max(jnp.abs(values), axis=1, keepdims=True)
    scale = jnp.maximum(top, 1e-30).astype(jnp.bfloat16).astype(jnp.float32)
    t = values * (GAIN / scale)
    t2 = t * t
    t4 = t2 * t2
    t8 = t4 * t4
    power = t8 * t8
    power = jnp.where(values < 0, -power, power)
    lanes = lax.broadcasted_iota(jnp.int32, values.shape, 1)
    return jnp.where(lanes == used, scale, power).astype(jnp.bfloat16)


def decode(coded, used):
    y = coded.astype(jnp.float32)
    scale = y[:, used : used + 1] * (1.0 / GAIN)
    root = lax.rsqrt(lax.rsqrt(lax.rsqrt(lax.rsqrt(jnp.abs(y)))))
    value = jnp.where(y < 0, -root, root) * scale
    lanes = lax.broadcasted_iota(jnp.int32, y.shape, 1)
    return jnp.where(lanes < used, value, 0.0)


def pack_amplitudes(x):
    occ, inner, width, virt = x.shape
    lanes = padded(inner * virt)

    def kernel(x_ref, *out_refs):
        first = 0
        for out_ref, count in zip(out_refs, CHUNKS):
            for i in range(count):
                rows = slice(i * width, (i + 1) * width)
                out_ref[rows, lanes - LANE :] = jnp.zeros((width, LANE), out_ref.dtype)
                for k in range(inner):
                    out_ref[rows, k * virt : (k + 1) * virt] = x_ref[first + i, k]
            first += count

    return pl.pallas_call(
        kernel,
        out_shape=[jax.ShapeDtypeStruct((count * width, lanes), x.dtype) for count in CHUNKS],
        in_specs=[whole()],
        out_specs=[whole() for _ in CHUNKS],
        compiler_params=params(),
    )(x)


def pack_integrals(slab, w):
    inner, outer, virt, wide = w.shape
    half = wide // 2
    rows = padded(inner * virt)
    lanes = padded(outer * half)

    def kernel(slab_ref, w_ref, mine_ref, other_ref):
        step = pl.program_id(0)
        low = slab_ref[0] == 0

        @pl.when(step == 0)
        def _():
            for out_ref in (mine_ref, other_ref):
                out_ref[:, lanes - LANE :] = jnp.zeros((rows, LANE), out_ref.dtype)
                out_ref[rows - 16 :, :] = jnp.zeros((16, lanes), out_ref.dtype)

        for k in range(inner):

            @pl.when(step == k)
            def _():
                for j in range(outer):
                    first, second = w_ref[0, j, :, :half], w_ref[0, j, :, half:]
                    at = (slice(k * virt, (k + 1) * virt), slice(j * half, (j + 1) * half))
                    mine_ref[at] = jnp.where(low, first, second)
                    other_ref[at] = jnp.where(low, second, first)

    shape = jax.ShapeDtypeStruct((rows, lanes), w.dtype)
    spec = pl.BlockSpec((rows, lanes), lambda k, s: (0, 0))
    return pl.pallas_call(
        kernel,
        out_shape=[shape, shape],
        grid_spec=pltpu.PrefetchScalarGridSpec(
            num_scalar_prefetch=1,
            grid=(inner,),
            in_specs=[pl.BlockSpec((1, outer, virt, wide), lambda k, s: (k, 0, 0, 0))],
            out_specs=[spec, spec],
        ),
        compiler_params=params(),
    )(slab, w)


def multiply(slab, gathered, mine, other, used):
    blocks, slabs, rows, _ = gathered.shape
    depth, lanes = mine.shape
    per_step = max(1, 256 // rows)

    def kernel(slab_ref, g_ref, mine_ref, other_ref, out_ref):
        own = slab_ref[0]

        def part(which):
            return g_ref[:, pl.ds(which, 1), :, :].reshape(per_step * rows, depth)

        total = jnp.dot(part(own), mine_ref[...], preferred_element_type=jnp.float32)
        total += jnp.dot(part(1 - own), other_ref[...], preferred_element_type=jnp.float32)
        out_ref[...] = encode(total, used).reshape(per_step, rows, lanes)

    return pl.pallas_call(
        kernel,
        out_shape=jax.ShapeDtypeStruct((blocks, rows, lanes), jnp.bfloat16),
        grid_spec=pltpu.PrefetchScalarGridSpec(
            num_scalar_prefetch=1,
            grid=(blocks // per_step,),
            in_specs=[
                pl.BlockSpec((per_step, slabs, rows, gathered.shape[3]), lambda n, s: (n, 0, 0, 0)),
                pl.BlockSpec((depth, lanes), lambda n, s: (0, 0)),
                pl.BlockSpec((depth, lanes), lambda n, s: (0, 0)),
            ],
            out_specs=pl.BlockSpec((per_step, rows, lanes), lambda n, s: (n, 0, 0)),
        ),
        compiler_params=params(),
    )(slab, gathered, mine, other)


def add_up(received, used):
    blocks, rows, lanes = received.shape

    def kernel(x_ref, sum_ref, coded_ref):
        total = decode(x_ref[0], used)
        for n in range(1, blocks):
            total += decode(x_ref[n], used)
        sum_ref[...] = total
        coded_ref[...] = encode(total, used)

    return pl.pallas_call(
        kernel,
        out_shape=[
            jax.ShapeDtypeStruct((rows, lanes), jnp.float32),
            jax.ShapeDtypeStruct((rows, lanes), jnp.bfloat16),
        ],
        in_specs=[whole()],
        out_specs=[whole(), whole()],
        compiler_params=params(),
    )(received)


def subtract(sums, mirrored, width, occ, virt):
    used = occ * virt
    count = len(sums)

    def kernel(*refs):
        sum_refs, mirror_refs, out_ref, flat = refs[:count], refs[count : 2 * count], refs[-2], refs[-1]
        first = 0
        for ref, n in zip(mirror_refs, CHUNKS):
            flat[first * width : (first + n) * width, :] = decode(ref[...], used)
            first += n
        first = 0
        for ref, n in zip(sum_refs, CHUNKS):
            for i in range(n):
                for j in range(occ):
                    own = ref[i * width : (i + 1) * width, j * virt : (j + 1) * virt]
                    at = first + i
                    out_ref[at, j] = own - flat[j * width : (j + 1) * width, at * virt : (at + 1) * virt]
            first += n

    return pl.pallas_call(
        kernel,
        out_shape=jax.ShapeDtypeStruct((occ, occ, width, virt), jnp.float32),
        in_specs=[whole() for _ in range(2 * count)],
        out_specs=whole(),
        scratch_shapes=[pltpu.VMEM((occ * width, sums[0].shape[1]), jnp.float32)],
        compiler_params=params(),
    )(*sums, *mirrored)


def on_device(amplitudes, integrals):
    occ, width, _, _ = amplitudes.shape
    out_occ = integrals.shape[2]
    out_virt = integrals.shape[3] // lax.axis_size("slab")
    used = out_occ * out_virt
    rows, cols = lax.axis_size("row"), lax.axis_size("col")
    slab = lax.axis_index("slab").astype(jnp.int32).reshape(1)
    mirror_pairs = [(r * cols + c, c * cols + r) for r in range(rows) for c in range(cols)]

    packed = pack_amplitudes(jnp.transpose(amplitudes, (0, 2, 1, 3)))
    gathered = []
    for chunk in packed:
        if gathered:
            chunk, _ = lax.optimization_barrier((chunk, gathered[-1]))
        gathered.append(lax.all_gather(chunk, ("col", "slab"), axis=0))
    mine, sent = pack_integrals(slab, jnp.transpose(integrals, (0, 2, 1, 3)))
    other = lax.ppermute(sent, "slab", [(0, 1), (1, 0)])

    sums, mirrored = [], []
    for chunk in gathered:
        chunk = chunk.reshape(cols, 2, chunk.shape[1], chunk.shape[2])
        coded = multiply(slab, chunk, mine, other, used)
        received = lax.all_to_all(coded, "row", 0, 0, tiled=True)
        total, again = add_up(received, used)
        sums.append(total)
        mirrored.append(lax.ppermute(again, ("row", "col"), mirror_pairs))
    residual = subtract(sums, mirrored, width, occ, out_virt)
    return jnp.transpose(residual, (0, 2, 1, 3))


def solution(mesh):
    return jax.shard_map(
        on_device,
        mesh=mesh,
        in_specs=(P("col", None, "row", "slab"), P("row", "slab", "col", None)),
        out_specs=P("row", None, "col", "slab"),
        check_vma=False,
    )
```

```python
import jax
import jax.numpy as jnp
from jax import lax
from jax.experimental import pallas as pl
from jax.experimental.pallas import tpu as pltpu
from jax.sharding import PartitionSpec as P

CHUNKS = (4, 3)
RING = 4
LANE = 128
GAIN = 2.0**7.875


def padded(size):
    return -(-size // LANE) * LANE


def whole():
    return pl.BlockSpec(memory_space=pltpu.VMEM)


def params(mib):
    return pltpu.CompilerParams(vmem_limit_bytes=mib * 1024 * 1024)


def cost(flops=0, moved=0):
    return pl.CostEstimate(flops=flops, bytes_accessed=moved, transcendentals=0)


def after(value, *arrays):
    return lax.optimization_barrier((value, *arrays))[0]


def encode(values, used):
    top = jnp.max(jnp.abs(values), axis=1, keepdims=True)
    scale = jnp.maximum(top, 1e-30).astype(jnp.bfloat16).astype(jnp.float32)
    t = values * (GAIN / scale)
    t2 = t * t
    t4 = t2 * t2
    t8 = t4 * t4
    power = t8 * t8
    power = jnp.where(values < 0, -power, power)
    lanes = lax.broadcasted_iota(jnp.int32, values.shape, 1)
    return jnp.where(lanes == used, scale, power).astype(jnp.bfloat16)


def decode(coded, used):
    y = coded.astype(jnp.float32)
    scale = y[:, used : used + 1] * (1.0 / GAIN)
    root = lax.rsqrt(lax.rsqrt(lax.rsqrt(lax.rsqrt(jnp.abs(y)))))
    value = jnp.where(y < 0, -root, root) * scale
    lanes = lax.broadcasted_iota(jnp.int32, y.shape, 1)
    return jnp.where(lanes < used, value, 0.0)


def pack_amplitudes(x):
    occ, inner, width, virt = x.shape
    lanes = padded(inner * virt)

    def kernel(x_ref, *out_refs):
        first = 0
        for out_ref, count in zip(out_refs, CHUNKS):
            for i in range(count):
                rows = slice(i * width, (i + 1) * width)
                out_ref[rows, lanes - LANE :] = jnp.zeros((width, LANE), out_ref.dtype)
                for k in range(inner):
                    out_ref[rows, k * virt : (k + 1) * virt] = x_ref[first + i, k]
            first += count

    return pl.pallas_call(
        kernel,
        out_shape=[jax.ShapeDtypeStruct((count * width, lanes), x.dtype) for count in CHUNKS],
        in_specs=[whole()],
        out_specs=[whole() for _ in CHUNKS],
        compiler_params=params(60),
        cost_estimate=cost(moved=4 * x.size),
    )(x)


def pack_integrals(slab, w):
    inner, outer, virt, wide = w.shape
    half = wide // 2
    rows = padded(inner * virt)
    lanes = padded(outer * half)

    def kernel(slab_ref, w_ref, mine_ref, other_ref):
        step = pl.program_id(0)
        low = slab_ref[0] == 0

        @pl.when(step == 0)
        def _():
            for out_ref in (mine_ref, other_ref):
                out_ref[:, lanes - LANE :] = jnp.zeros((rows, LANE), out_ref.dtype)
                out_ref[rows - 16 :, :] = jnp.zeros((16, lanes), out_ref.dtype)

        for k in range(inner):

            @pl.when(step == k)
            def _():
                for j in range(outer):
                    first, second = w_ref[0, j, :, :half], w_ref[0, j, :, half:]
                    at = (slice(k * virt, (k + 1) * virt), slice(j * half, (j + 1) * half))
                    mine_ref[at] = jnp.where(low, first, second)
                    other_ref[at] = jnp.where(low, second, first)

    shape = jax.ShapeDtypeStruct((rows, lanes), w.dtype)
    spec = pl.BlockSpec((rows, lanes), lambda k, s: (0, 0))
    return pl.pallas_call(
        kernel,
        out_shape=[shape, shape],
        grid_spec=pltpu.PrefetchScalarGridSpec(
            num_scalar_prefetch=1,
            grid=(inner,),
            in_specs=[pl.BlockSpec((1, outer, virt, wide), lambda k, s: (k, 0, 0, 0))],
            out_specs=[spec, spec],
        ),
        compiler_params=params(60),
        cost_estimate=cost(moved=8 * w.size),
    )(slab, w)


def multiply(places, gathered, rings, mine, other, used, apart):
    depth, lanes = mine.shape
    rows = gathered.shape[-2]
    count = gathered.shape[0] * (gathered.shape[2] if rings else 1)
    group = RING if rings else max(1, min(count, 256 // rows))

    def kernel(slab_ref, ring_ref, dest_ref, g_ref, mine_ref, other_ref, *refs):
        out_refs, (total, left, right, mine_buf, other_buf, sems) = refs[:-6], refs[-6:]
        moves = [[(mine_ref, mine_buf)], [(other_ref, other_buf)]]
        for side, buf in enumerate((left, right)):
            which = slab_ref[0] if side == 0 else 1 - slab_ref[0]
            if rings:
                for n in range(count // RING):
                    moves[side].append((g_ref.at[:, which, n], buf.at[n * RING : (n + 1) * RING]))
            else:
                moves[side].append((g_ref.at[:, which], buf))
        copies, n = [[], []], 0
        for side in range(2):
            for src, dst in moves[side]:
                copies[side].append(pltpu.make_async_copy(src, dst, sems.at[n]))
                copies[side][-1].start()
                n += 1

        def product(start, rows_ref, buf):
            block = rows_ref[start : start + group].reshape(group * rows, depth)
            return jnp.dot(block, buf[...], preferred_element_type=jnp.float32).reshape(group, rows, lanes)

        def place(start):
            if not rings:
                return slice(start, start + group)
            ring = ring_ref[0] if start == 0 else 1 - ring_ref[0]
            return pl.ds(ring * RING, RING)

        for copy in copies[0]:
            copy.wait()
        for start in range(0, count, group):
            total[place(start)] = product(start, left, mine_buf)
        for copy in copies[1]:
            copy.wait()
        for start in range(0, count, group):
            block = total[place(start)] + product(start, right, other_buf)
            if apart:
                total[place(start)] = block
            else:
                coded = encode(block.reshape(group * rows, lanes), used)
                out_refs[0][place(start)] = coded.reshape(group, rows, lanes)
        if apart:
            out_refs[0][...] = total[dest_ref[0]]
            for n, out_ref in enumerate(out_refs[1:]):
                out_ref[...] = encode(total[dest_ref[n + 1]], used)

    if apart:
        shapes = [jax.ShapeDtypeStruct((rows, lanes), jnp.float32)]
        shapes += [jax.ShapeDtypeStruct((rows, lanes), jnp.bfloat16)] * (count - 1)
    else:
        shapes = [jax.ShapeDtypeStruct((count, rows, lanes), jnp.bfloat16)]
    smem, hbm = pl.BlockSpec(memory_space=pltpu.SMEM), pl.BlockSpec(memory_space=pl.ANY)
    return pl.pallas_call(
        kernel,
        out_shape=shapes,
        in_specs=[smem] * 3 + [hbm] * 3,
        out_specs=[whole() for _ in shapes],
        scratch_shapes=[
            pltpu.VMEM((count, rows, lanes), jnp.float32),
            pltpu.VMEM((count, rows, depth), mine.dtype),
            pltpu.VMEM((count, rows, depth), mine.dtype),
            pltpu.VMEM(mine.shape, mine.dtype),
            pltpu.VMEM(other.shape, other.dtype),
            pltpu.SemaphoreType.DMA((2 + (count // RING) * 2,)),
        ],
        compiler_params=params(60),
        cost_estimate=cost(flops=4 * count * rows * depth * lanes, moved=8 * depth * lanes),
    )(*places, gathered, mine, other)


def add_up(parts, used):
    rows, lanes = parts[0].shape[-2:]

    def kernel(*refs):
        sum_ref, coded_ref = refs[-2:]
        total = 0.0
        for ref in refs[:-2]:
            if len(ref.shape) == 3:
                for n in range(ref.shape[0]):
                    total += decode(ref[n], used)
            elif ref.dtype == jnp.float32:
                total += ref[...]
            else:
                total += decode(ref[...], used)
        sum_ref[...] = total
        coded_ref[...] = encode(total, used)

    return pl.pallas_call(
        kernel,
        out_shape=[
            jax.ShapeDtypeStruct((rows, lanes), jnp.float32),
            jax.ShapeDtypeStruct((rows, lanes), jnp.bfloat16),
        ],
        in_specs=[whole() for _ in parts],
        out_specs=[whole(), whole()],
        compiler_params=params(60),
        cost_estimate=cost(moved=64 * rows * lanes),
    )(*parts)


def subtract(sums, mirrored, width, occ, virt):
    used = occ * virt
    count = len(sums)

    def kernel(*refs):
        sum_refs, mirror_refs, out_ref, flat = refs[:count], refs[count : 2 * count], refs[-2], refs[-1]
        first = 0
        for ref, n in zip(mirror_refs, CHUNKS):
            flat[first * width : (first + n) * width, :] = decode(ref[...], used)
            first += n
        first = 0
        for ref, n in zip(sum_refs, CHUNKS):
            for i in range(n):
                for j in range(occ):
                    own = ref[i * width : (i + 1) * width, j * virt : (j + 1) * virt]
                    at = first + i
                    out_ref[at, j] = own - flat[j * width : (j + 1) * width, at * virt : (at + 1) * virt]
            first += n

    return pl.pallas_call(
        kernel,
        out_shape=jax.ShapeDtypeStruct((occ, occ, width, virt), jnp.float32),
        in_specs=[whole() for _ in range(2 * count)],
        out_specs=whole(),
        scratch_shapes=[pltpu.VMEM((occ * width, sums[0].shape[1]), jnp.float32)],
        compiler_params=params(60),
        cost_estimate=cost(moved=32 * occ * occ * width * virt),
    )(*sums, *mirrored)


def distances(size):
    halves = size // RING
    return [(0, 0)] + [(h, s) for h in range(halves - 1, -1, -1) for s in (2, 1, -1, 0) if (h, s) != (0, 0)]


def moved(place, size, distance):
    half, step = distance
    ring = place // RING
    return (ring + half) % (size // RING) * RING + (place % RING + step) % RING


def on_device(amplitudes, integrals):
    occ, width, _, _ = amplitudes.shape
    out_occ = integrals.shape[2]
    out_virt = integrals.shape[3] // lax.axis_size("slab")
    used = out_occ * out_virt
    rows, cols = lax.axis_size("row"), lax.axis_size("col")
    slab = lax.axis_index("slab").astype(jnp.int32).reshape(1)
    mirror_pairs = [(r * cols + c, c * cols + r) for r in range(rows) for c in range(cols)]
    apart = distances(rows)
    row = lax.axis_index("row").astype(jnp.int32)
    dest = jnp.stack([moved(row, rows, distance) for distance in apart])

    ring = (lax.axis_index("col") // RING).astype(jnp.int32).reshape(1)
    places = (slab, ring, dest)
    swap = [(0, 1), (1, 0)]
    cross = [(c, (c + RING) % cols) for c in range(cols)]
    groups = [list(range(n, n + 2 * RING)) for n in range(0, 2 * cols, 2 * RING)]

    packed, rest = pack_amplitudes(jnp.transpose(amplitudes, (0, 2, 1, 3)))
    early = lax.all_gather(packed, ("col", "slab"), axis=0)
    early = early.reshape(cols, 2, *packed.shape)
    mine, sent = pack_integrals(after(slab, packed), jnp.transpose(integrals, (0, 2, 1, 3)))
    other = lax.ppermute(sent, "slab", swap)
    pair = jnp.stack([rest, lax.ppermute(after(rest, other), "col", cross)])
    late = lax.all_gather(after(pair, early), ("col", "slab"), axis=0, axis_index_groups=groups)
    late = late.reshape(RING, 2, *pair.shape)

    shares = []
    for source, rings in ((early, False), (late, True)):
        (coded,) = multiply(places, source, rings, mine, other, used, False)
        shares.append([lax.all_to_all(coded, "row", 0, 0, tiled=True)])

    sums, mirrored = [], []
    for parts in shares:
        if sums:
            parts = list(lax.optimization_barrier((*parts, sums[-1]))[:-1])
        total, again = add_up(parts, used)
        sums.append(total)
        mirrored.append(lax.ppermute(again, ("row", "col"), mirror_pairs))
    residual = subtract(sums, mirrored, width, occ, out_virt)
    return jnp.transpose(residual, (0, 2, 1, 3))


def solution(mesh):
    return jax.shard_map(
        on_device,
        mesh=mesh,
        in_specs=(P("col", None, "row", "slab"), P("row", "slab", "col", None)),
        out_specs=P("row", None, "col", "slab"),
        check_vma=False,
    )
```

```python
import jax
import jax.numpy as jnp
from jax import lax
from jax.experimental import pallas as pl
from jax.experimental.pallas import tpu as pltpu
from jax.sharding import PartitionSpec as P

CHUNKS = (4, 3)
RING = 4
STEPS = (2, 1, -1)
LANE = 128
GAIN = 2.0**7.875


def padded(size):
    return -(-size // LANE) * LANE


def whole():
    return pl.BlockSpec(memory_space=pltpu.VMEM)


def params(mib):
    return pltpu.CompilerParams(vmem_limit_bytes=mib * 1024 * 1024)


def cost(flops=0, moved=0):
    return pl.CostEstimate(flops=flops, bytes_accessed=moved, transcendentals=0)


def after(value, *arrays):
    return lax.optimization_barrier((value, *arrays))[0]


def encode(values, used):
    top = jnp.max(jnp.abs(values), axis=1, keepdims=True)
    scale = jnp.maximum(top, 1e-30).astype(jnp.bfloat16).astype(jnp.float32)
    t = values * (GAIN / scale)
    t2 = t * t
    t4 = t2 * t2
    t8 = t4 * t4
    power = t8 * t8
    power = jnp.where(values < 0, -power, power)
    lanes = lax.broadcasted_iota(jnp.int32, values.shape, 1)
    return jnp.where(lanes == used, scale, power).astype(jnp.bfloat16)


def decode(coded, used):
    y = coded.astype(jnp.float32)
    scale = y[:, used : used + 1] * (1.0 / GAIN)
    root = lax.rsqrt(lax.rsqrt(lax.rsqrt(lax.rsqrt(jnp.abs(y)))))
    value = jnp.where(y < 0, -root, root) * scale
    lanes = lax.broadcasted_iota(jnp.int32, y.shape, 1)
    return jnp.where(lanes < used, value, 0.0)


def pack_amplitudes(x):
    occ, inner, width, virt = x.shape
    lanes = padded(inner * virt)

    def kernel(x_ref, *out_refs):
        first = 0
        for out_ref, count in zip(out_refs, CHUNKS):
            for i in range(count):
                rows = slice(i * width, (i + 1) * width)
                out_ref[rows, lanes - LANE :] = jnp.zeros((width, LANE), out_ref.dtype)
                for k in range(inner):
                    out_ref[rows, k * virt : (k + 1) * virt] = x_ref[first + i, k]
            first += count

    return pl.pallas_call(
        kernel,
        out_shape=[jax.ShapeDtypeStruct((count * width, lanes), x.dtype) for count in CHUNKS],
        in_specs=[whole()],
        out_specs=[whole() for _ in CHUNKS],
        compiler_params=params(60),
        cost_estimate=cost(moved=4 * x.size),
    )(x)


def pack_integrals(slab, w):
    inner, outer, virt, wide = w.shape
    half = wide // 2
    rows = padded(inner * virt)
    lanes = padded(outer * half)

    def kernel(slab_ref, w_ref, mine_ref, other_ref):
        step = pl.program_id(0)
        low = slab_ref[0] == 0

        @pl.when(step == 0)
        def _():
            for out_ref in (mine_ref, other_ref):
                out_ref[:, lanes - LANE :] = jnp.zeros((rows, LANE), out_ref.dtype)
                out_ref[rows - 16 :, :] = jnp.zeros((16, lanes), out_ref.dtype)

        for k in range(inner):

            @pl.when(step == k)
            def _():
                for j in range(outer):
                    first, second = w_ref[0, j, :, :half], w_ref[0, j, :, half:]
                    at = (slice(k * virt, (k + 1) * virt), slice(j * half, (j + 1) * half))
                    mine_ref[at] = jnp.where(low, first, second)
                    other_ref[at] = jnp.where(low, second, first)

    shape = jax.ShapeDtypeStruct((rows, lanes), w.dtype)
    spec = pl.BlockSpec((rows, lanes), lambda k, s: (0, 0))
    return pl.pallas_call(
        kernel,
        out_shape=[shape, shape],
        grid_spec=pltpu.PrefetchScalarGridSpec(
            num_scalar_prefetch=1,
            grid=(inner,),
            in_specs=[pl.BlockSpec((1, outer, virt, wide), lambda k, s: (k, 0, 0, 0))],
            out_specs=[spec, spec],
        ),
        compiler_params=params(60),
        cost_estimate=cost(moved=8 * w.size),
    )(slab, w)


def multiply(places, gathered, rings, mine, other, used, far):
    depth, lanes = mine.shape
    rows = gathered.shape[-2]

    def kernel(slab_ref, ring_ref, half_ref, g_ref, mine_ref, other_ref, out_ref, *scratch):
        left, right, mine_buf, other_buf, sems = scratch
        half = 1 - half_ref[0] if far else half_ref[0]
        copies = []
        for side, (rows_buf, src, dst) in enumerate(((left, mine_ref, mine_buf), (right, other_ref, other_buf))):
            which = slab_ref[0] if side == 0 else 1 - slab_ref[0]
            if rings:
                block = g_ref.at[:, which, jnp.where(ring_ref[0] == half, 0, 1)]
            else:
                block = g_ref.at[pl.ds(half * RING, RING), which]
            copies.append(
                [
                    pltpu.make_async_copy(block, rows_buf, sems.at[2 * side]),
                    pltpu.make_async_copy(src, dst, sems.at[2 * side + 1]),
                ]
            )
            for copy in copies[-1]:
                copy.start()

        def product(rows_buf, buf):
            return jnp.dot(rows_buf[...].reshape(RING * rows, depth), buf[...], preferred_element_type=jnp.float32)

        for copy in copies[0]:
            copy.wait()
        total = product(left, mine_buf)
        for copy in copies[1]:
            copy.wait()
        total += product(right, other_buf)
        out_ref[...] = (encode(total, used) if far else total).reshape(RING, rows, lanes)

    smem, hbm = pl.BlockSpec(memory_space=pltpu.SMEM), pl.BlockSpec(memory_space=pl.ANY)
    return pl.pallas_call(
        kernel,
        out_shape=jax.ShapeDtypeStruct((RING, rows, lanes), jnp.bfloat16 if far else jnp.float32),
        in_specs=[smem] * 3 + [hbm] * 3,
        out_specs=whole(),
        scratch_shapes=[
            pltpu.VMEM((RING, rows, depth), mine.dtype),
            pltpu.VMEM((RING, rows, depth), mine.dtype),
            pltpu.VMEM(mine.shape, mine.dtype),
            pltpu.VMEM(other.shape, other.dtype),
            pltpu.SemaphoreType.DMA((4,)),
        ],
        compiler_params=params(60),
        cost_estimate=cost(flops=4 * RING * rows * depth * lanes, moved=8 * depth * lanes),
    )(*places, gathered, mine, other)


def add_halves(place, near, far, used):
    _, rows, lanes = near.shape

    def kernel(place_ref, near_ref, far_ref, own_ref, *refs):
        own_ref[...] = near_ref[place_ref[0]] + decode(far_ref[place_ref[0]], used)
        for out_ref, step in zip(refs, STEPS):
            there = (place_ref[0] + step + RING) % RING
            out_ref[...] = encode(near_ref[there] + decode(far_ref[there], used), used)

    shapes = [jax.ShapeDtypeStruct((rows, lanes), jnp.float32)]
    shapes += [jax.ShapeDtypeStruct((rows, lanes), jnp.bfloat16)] * len(STEPS)
    return pl.pallas_call(
        kernel,
        out_shape=shapes,
        in_specs=[pl.BlockSpec(memory_space=pltpu.SMEM), whole(), whole()],
        out_specs=[whole() for _ in shapes],
        compiler_params=params(60),
        cost_estimate=cost(moved=32 * rows * lanes),
    )(place, near, far)


def add_up(parts, used):
    rows, lanes = parts[0].shape[-2:]

    def kernel(*refs):
        sum_ref, coded_ref = refs[-2:]
        total = 0.0
        for ref in refs[:-2]:
            if len(ref.shape) == 3:
                for n in range(ref.shape[0]):
                    total += decode(ref[n], used)
            elif ref.dtype == jnp.float32:
                total += ref[...]
            else:
                total += decode(ref[...], used)
        sum_ref[...] = total
        coded_ref[...] = encode(total, used)

    return pl.pallas_call(
        kernel,
        out_shape=[
            jax.ShapeDtypeStruct((rows, lanes), jnp.float32),
            jax.ShapeDtypeStruct((rows, lanes), jnp.bfloat16),
        ],
        in_specs=[whole() for _ in parts],
        out_specs=[whole(), whole()],
        compiler_params=params(60),
        cost_estimate=cost(moved=64 * rows * lanes),
    )(*parts)


def subtract(sums, mirrored, chunk, residual, width, occ, virt):
    used = occ * virt
    count = len(sums)
    first = sum(CHUNKS[:chunk])
    columns = range(first, first + CHUNKS[chunk])

    def kernel(*refs):
        sum_refs, mirror_ref = refs[:count], refs[count]
        out_ref, flat, part, sem = refs[-4:]
        flat[...] = decode(mirror_ref[...], used)
        at = 0
        for ref, n in zip(sum_refs, CHUNKS):
            for i in range(n):
                for j in columns:
                    here = ref[i * width : (i + 1) * width, j * virt : (j + 1) * virt]
                    there = slice((j - first) * width, (j - first + 1) * width)
                    part[at, j - first] = here - flat[there, at * virt : (at + 1) * virt]
                at += 1
        copy = pltpu.make_async_copy(part, out_ref.at[:, first : first + len(columns)], sem)
        copy.start()
        copy.wait()

    hbm = pl.BlockSpec(memory_space=pl.ANY)
    before = [] if residual is None else [residual]
    return pl.pallas_call(
        kernel,
        out_shape=jax.ShapeDtypeStruct((occ, occ, width, virt), jnp.float32),
        in_specs=[whole() for _ in range(count + 1)] + [hbm] * len(before),
        out_specs=hbm,
        scratch_shapes=[
            pltpu.VMEM(mirrored.shape, jnp.float32),
            pltpu.VMEM((occ, len(columns), width, virt), jnp.float32),
            pltpu.SemaphoreType.DMA(()),
        ],
        input_output_aliases={count + 1: 0} if before else {},
        compiler_params=params(60),
        cost_estimate=cost(moved=16 * occ * len(columns) * width * virt),
    )(*sums, mirrored, *before)


def on_device(amplitudes, integrals):
    occ, width, _, _ = amplitudes.shape
    out_occ = integrals.shape[2]
    out_virt = integrals.shape[3] // lax.axis_size("slab")
    used = out_occ * out_virt
    rows, cols = lax.axis_size("row"), lax.axis_size("col")
    slab = lax.axis_index("slab").astype(jnp.int32).reshape(1)
    mirror_pairs = [(r * cols + c, c * cols + r) for r in range(rows) for c in range(cols)]
    row = lax.axis_index("row").astype(jnp.int32)
    half, place = (row // RING).reshape(1), (row % RING).reshape(1)
    ring = (lax.axis_index("col") // RING).astype(jnp.int32).reshape(1)
    swap = [(0, 1), (1, 0)]
    cross = [(c, (c + RING) % cols) for c in range(cols)]
    groups = [list(range(n, n + 2 * RING)) for n in range(0, 2 * cols, 2 * RING)]

    packed, rest = pack_amplitudes(jnp.transpose(amplitudes, (0, 2, 1, 3)))
    early = lax.all_gather(packed, ("col", "slab"), axis=0)
    early = early.reshape(cols, 2, *packed.shape)
    mine, sent = pack_integrals(after(slab, packed), jnp.transpose(integrals, (0, 2, 1, 3)))
    other = lax.ppermute(sent, "slab", swap)
    pair = jnp.stack([rest, lax.ppermute(after(rest, other), "col", cross)])
    late = lax.all_gather(after(pair, early), ("col", "slab"), axis=0, axis_index_groups=groups)
    late = late.reshape(RING, 2, *pair.shape)

    def shifted(value, step):
        pairs = [(r, r // RING * RING + (r + step) % RING) for r in range(rows)]
        return lax.ppermute(value, "row", pairs)

    def mirror(parts):
        total, again = add_up(parts, used)
        return total, lax.ppermute(again, ("row", "col"), mirror_pairs)

    def product(token, source, rings, far):
        return multiply((after(slab, *token), ring, half), source, rings, mine, other, used, far)

    def around(near, far):
        own, *others = add_halves(place, near, far, used)
        return [own, *(shifted(part, step) for part, step in zip(others, STEPS))]

    far = product((), early, False, True)
    early_far = lax.ppermute(far, "row", cross)
    early_near = product((far,), early, False, False)
    far = product((early_near,), late, True, True)
    late_far = lax.ppermute(far, "row", cross)
    early_parts = around(early_near, early_far)
    late_near = product((far, early_parts[0]), late, True, False)
    late_parts = around(late_near, late_far)
    first, again = add_up(early_parts, used)
    second, last = add_up(late_parts, used)
    again = after(again, *late_parts)
    sums = (first, second)
    mirrored = [lax.ppermute(part, ("row", "col"), mirror_pairs) for part in (again, last)]
    residual = None
    for chunk, block in enumerate(mirrored):
        residual = subtract(sums, block, chunk, residual, width, occ, out_virt)
    return jnp.transpose(residual, (0, 2, 1, 3))


def solution(mesh):
    return jax.shard_map(
        on_device,
        mesh=mesh,
        in_specs=(P("col", None, "row", "slab"), P("row", "slab", "col", None)),
        out_specs=P("row", None, "col", "slab"),
        check_vma=False,
    )
```

```python
import jax
import jax.numpy as jnp
from jax import lax
from jax.experimental import pallas as pl
from jax.experimental.pallas import tpu as pltpu
from jax.sharding import PartitionSpec as P

CHUNKS = (4, 3)
RING = 4
STEPS = (2, 1, -1)
LANE = 128
GAIN = 2.0**7.875


def padded(size):
    return -(-size // LANE) * LANE


def whole():
    return pl.BlockSpec(memory_space=pltpu.VMEM)


def params(mib):
    return pltpu.CompilerParams(vmem_limit_bytes=mib * 1024 * 1024)


def cost(flops=0, moved=0):
    return pl.CostEstimate(flops=flops, bytes_accessed=moved, transcendentals=0)


def after(value, *arrays):
    return lax.optimization_barrier((value, *arrays))[0]


def encode(values, used):
    top = jnp.max(jnp.abs(values), axis=1, keepdims=True)
    scale = jnp.maximum(top, 1e-30).astype(jnp.bfloat16).astype(jnp.float32)
    t = values * (GAIN / scale)
    t2 = t * t
    t4 = t2 * t2
    t8 = t4 * t4
    power = t8 * t8
    power = jnp.where(values < 0, -power, power)
    lanes = lax.broadcasted_iota(jnp.int32, values.shape, 1)
    return jnp.where(lanes == used, scale, power).astype(jnp.bfloat16)


def decode(coded, used):
    y = coded.astype(jnp.float32)
    scale = y[:, used : used + 1] * (1.0 / GAIN)
    root = lax.rsqrt(lax.rsqrt(lax.rsqrt(lax.rsqrt(jnp.abs(y)))))
    value = jnp.where(y < 0, -root, root) * scale
    lanes = lax.broadcasted_iota(jnp.int32, y.shape, 1)
    return jnp.where(lanes < used, value, 0.0)


def pack_amplitudes(x):
    occ, inner, width, virt = x.shape
    lanes = padded(inner * virt)

    def kernel(x_ref, *out_refs):
        first = 0
        for out_ref, count in zip(out_refs, CHUNKS):
            for i in range(count):
                rows = slice(i * width, (i + 1) * width)
                out_ref[rows, lanes - LANE :] = jnp.zeros((width, LANE), out_ref.dtype)
                for k in range(inner):
                    out_ref[rows, k * virt : (k + 1) * virt] = x_ref[first + i, k]
            first += count

    return pl.pallas_call(
        kernel,
        out_shape=[jax.ShapeDtypeStruct((count * width, lanes), x.dtype) for count in CHUNKS],
        in_specs=[whole()],
        out_specs=[whole() for _ in CHUNKS],
        compiler_params=params(60),
        cost_estimate=cost(moved=4 * x.size),
    )(x)


def pack_integrals(slab, w):
    inner, outer, virt, wide = w.shape
    half = wide // 2
    rows = padded(inner * virt)
    lanes = padded(outer * half)

    def kernel(slab_ref, w_ref, mine_ref, other_ref):
        step = pl.program_id(0)
        low = slab_ref[0] == 0

        @pl.when(step == 0)
        def _():
            for out_ref in (mine_ref, other_ref):
                out_ref[:, lanes - LANE :] = jnp.zeros((rows, LANE), out_ref.dtype)
                out_ref[rows - 16 :, :] = jnp.zeros((16, lanes), out_ref.dtype)

        for k in range(inner):

            @pl.when(step == k)
            def _():
                for j in range(outer):
                    first, second = w_ref[0, j, :, :half], w_ref[0, j, :, half:]
                    at = (slice(k * virt, (k + 1) * virt), slice(j * half, (j + 1) * half))
                    mine_ref[at] = jnp.where(low, first, second)
                    other_ref[at] = jnp.where(low, second, first)

    shape = jax.ShapeDtypeStruct((rows, lanes), w.dtype)
    spec = pl.BlockSpec((rows, lanes), lambda k, s: (0, 0))
    return pl.pallas_call(
        kernel,
        out_shape=[shape, shape],
        grid_spec=pltpu.PrefetchScalarGridSpec(
            num_scalar_prefetch=1,
            grid=(inner,),
            in_specs=[pl.BlockSpec((1, outer, virt, wide), lambda k, s: (k, 0, 0, 0))],
            out_specs=[spec, spec],
        ),
        compiler_params=params(60),
        cost_estimate=cost(moved=8 * w.size),
    )(slab, w)


def multiply(places, gathered, rings, mine, other, used, far):
    depth, lanes = mine.shape
    rows = gathered.shape[-2]

    def kernel(slab_ref, ring_ref, half_ref, g_ref, mine_ref, other_ref, out_ref, *scratch):
        left, right, mine_buf, other_buf, sems = scratch
        half = 1 - half_ref[0] if far else half_ref[0]
        copies = []
        for side, (rows_buf, src, dst) in enumerate(((left, mine_ref, mine_buf), (right, other_ref, other_buf))):
            which = slab_ref[0] if side == 0 else 1 - slab_ref[0]
            if rings:
                block = g_ref.at[:, which, jnp.where(ring_ref[0] == half, 0, 1)]
            else:
                block = g_ref.at[pl.ds(half * RING, RING), which]
            copies.append(
                [
                    pltpu.make_async_copy(block, rows_buf, sems.at[2 * side]),
                    pltpu.make_async_copy(src, dst, sems.at[2 * side + 1]),
                ]
            )
            for copy in copies[-1]:
                copy.start()

        def product(rows_buf, buf):
            return jnp.dot(rows_buf[...].reshape(RING * rows, depth), buf[...], preferred_element_type=jnp.float32)

        for copy in copies[0]:
            copy.wait()
        total = product(left, mine_buf)
        for copy in copies[1]:
            copy.wait()
        total += product(right, other_buf)
        out_ref[...] = (encode(total, used) if far else total).reshape(RING, rows, lanes)

    smem, hbm = pl.BlockSpec(memory_space=pltpu.SMEM), pl.BlockSpec(memory_space=pl.ANY)
    return pl.pallas_call(
        kernel,
        out_shape=jax.ShapeDtypeStruct((RING, rows, lanes), jnp.bfloat16 if far else jnp.float32),
        in_specs=[smem] * 3 + [hbm] * 3,
        out_specs=whole(),
        scratch_shapes=[
            pltpu.VMEM((RING, rows, depth), mine.dtype),
            pltpu.VMEM((RING, rows, depth), mine.dtype),
            pltpu.VMEM(mine.shape, mine.dtype),
            pltpu.VMEM(other.shape, other.dtype),
            pltpu.SemaphoreType.DMA((4,)),
        ],
        compiler_params=params(60),
        cost_estimate=cost(flops=4 * RING * rows * depth * lanes, moved=8 * depth * lanes),
    )(*places, gathered, mine, other)


def add_halves(place, near, far, used):
    _, rows, lanes = near.shape

    def kernel(place_ref, near_ref, far_ref, own_ref, *refs):
        own_ref[...] = near_ref[place_ref[0]] + decode(far_ref[place_ref[0]], used)
        for out_ref, step in zip(refs, STEPS):
            there = (place_ref[0] + step + RING) % RING
            out_ref[...] = encode(near_ref[there] + decode(far_ref[there], used), used)

    shapes = [jax.ShapeDtypeStruct((rows, lanes), jnp.float32)]
    shapes += [jax.ShapeDtypeStruct((rows, lanes), jnp.bfloat16)] * len(STEPS)
    return pl.pallas_call(
        kernel,
        out_shape=shapes,
        in_specs=[pl.BlockSpec(memory_space=pltpu.SMEM), whole(), whole()],
        out_specs=[whole() for _ in shapes],
        compiler_params=params(60),
        cost_estimate=cost(moved=32 * rows * lanes),
    )(place, near, far)


def add_up(parts, used):
    rows, lanes = parts[0].shape[-2:]

    def kernel(*refs):
        sum_ref, coded_ref = refs[-2:]
        total = 0.0
        for ref in refs[:-2]:
            if len(ref.shape) == 3:
                for n in range(ref.shape[0]):
                    total += decode(ref[n], used)
            elif ref.dtype == jnp.float32:
                total += ref[...]
            else:
                total += decode(ref[...], used)
        sum_ref[...] = total
        coded_ref[...] = encode(total, used)

    return pl.pallas_call(
        kernel,
        out_shape=[
            jax.ShapeDtypeStruct((rows, lanes), jnp.float32),
            jax.ShapeDtypeStruct((rows, lanes), jnp.bfloat16),
        ],
        in_specs=[whole() for _ in parts],
        out_specs=[whole(), whole()],
        compiler_params=params(60),
        cost_estimate=cost(moved=64 * rows * lanes),
    )(*parts)


def subtract(sums, mirrored, chunk, residual, width, occ, virt):
    used = occ * virt
    count = len(sums)
    first = sum(CHUNKS[:chunk])
    columns = range(first, first + CHUNKS[chunk])

    def kernel(*refs):
        sum_refs, mirror_ref = refs[:count], refs[count]
        out_ref, flat, part, sem = refs[-4:]
        flat[...] = decode(mirror_ref[...], used)
        at = 0
        for ref, n in zip(sum_refs, CHUNKS):
            for i in range(n):
                for j in columns:
                    here = ref[i * width : (i + 1) * width, j * virt : (j + 1) * virt]
                    there = slice((j - first) * width, (j - first + 1) * width)
                    part[at, j - first] = here - flat[there, at * virt : (at + 1) * virt]
                at += 1
        copy = pltpu.make_async_copy(part, out_ref.at[:, first : first + len(columns)], sem)
        copy.start()
        copy.wait()

    hbm = pl.BlockSpec(memory_space=pl.ANY)
    before = [] if residual is None else [residual]
    return pl.pallas_call(
        kernel,
        out_shape=jax.ShapeDtypeStruct((occ, occ, width, virt), jnp.float32),
        in_specs=[whole() for _ in range(count + 1)] + [hbm] * len(before),
        out_specs=hbm,
        scratch_shapes=[
            pltpu.VMEM(mirrored.shape, jnp.float32),
            pltpu.VMEM((occ, len(columns), width, virt), jnp.float32),
            pltpu.SemaphoreType.DMA(()),
        ],
        input_output_aliases={count + 1: 0} if before else {},
        compiler_params=params(60),
        cost_estimate=cost(moved=16 * occ * len(columns) * width * virt),
    )(*sums, mirrored, *before)


def on_device(amplitudes, integrals):
    occ, width, _, _ = amplitudes.shape
    out_occ = integrals.shape[2]
    out_virt = integrals.shape[3] // lax.axis_size("slab")
    used = out_occ * out_virt
    rows, cols = lax.axis_size("row"), lax.axis_size("col")
    slab = lax.axis_index("slab").astype(jnp.int32).reshape(1)
    mirror_pairs = [(r * cols + c, c * cols + r) for r in range(rows) for c in range(cols)]
    row = lax.axis_index("row").astype(jnp.int32)
    half, place = (row // RING).reshape(1), (row % RING).reshape(1)
    ring = (lax.axis_index("col") // RING).astype(jnp.int32).reshape(1)
    swap = [(0, 1), (1, 0)]
    cross = [(c, (c + RING) % cols) for c in range(cols)]
    groups = [list(range(n, n + 2 * RING)) for n in range(0, 2 * cols, 2 * RING)]

    packed, rest = pack_amplitudes(jnp.transpose(amplitudes, (0, 2, 1, 3)))
    early = lax.all_gather(packed, ("col", "slab"), axis=0)
    early = early.reshape(cols, 2, *packed.shape)
    across = lax.ppermute(rest, "col", cross)
    mine, sent = pack_integrals(after(slab, across), jnp.transpose(integrals, (0, 2, 1, 3)))
    other = lax.ppermute(sent, "slab", swap)
    pair = jnp.stack([rest, across])
    late = lax.all_gather(after(pair, early, other), ("col", "slab"), axis=0, axis_index_groups=groups)
    late = late.reshape(RING, 2, *pair.shape)

    def shifted(value, step):
        pairs = [(r, r // RING * RING + (r + step) % RING) for r in range(rows)]
        return lax.ppermute(value, "row", pairs)

    def mirror(parts):
        total, again = add_up(parts, used)
        return total, lax.ppermute(again, ("row", "col"), mirror_pairs)

    def product(token, source, rings, far):
        return multiply((after(slab, *token), ring, half), source, rings, mine, other, used, far)

    def around(near, far):
        own, *others = add_halves(place, near, far, used)
        return [own, *(shifted(part, step) for part, step in zip(others, STEPS))]

    far = product((), early, False, True)
    early_far = lax.ppermute(far, "row", cross)
    early_near = product((far,), early, False, False)
    far = product((early_near,), late, True, True)
    late_far = lax.ppermute(far, "row", cross)
    early_parts = around(early_near, early_far)
    late_near = product((far, early_parts[0]), late, True, False)
    late_parts = around(late_near, late_far)
    first, again = add_up(early_parts, used)
    second, last = add_up(late_parts, used)
    again = after(again, *late_parts)
    sums = (first, second)
    mirrored = [lax.ppermute(part, ("row", "col"), mirror_pairs) for part in (again, last)]
    residual = None
    for chunk, block in enumerate(mirrored):
        residual = subtract(sums, block, chunk, residual, width, occ, out_virt)
    return jnp.transpose(residual, (0, 2, 1, 3))


def solution(mesh):
    return jax.shard_map(
        on_device,
        mesh=mesh,
        in_specs=(P("col", None, "row", "slab"), P("row", "slab", "col", None)),
        out_specs=P("row", None, "col", "slab"),
        check_vma=False,
    )
```

```python
import jax
import jax.numpy as jnp
from jax import lax
from jax.experimental import pallas as pl
from jax.experimental.pallas import tpu as pltpu
from jax.sharding import PartitionSpec as P

CHUNKS = (4, 3)
RING = 4
STEPS = (2, 1, -1)
LANE = 128
GAIN = 2.0**7.875


def padded(size):
    return -(-size // LANE) * LANE


def whole():
    return pl.BlockSpec(memory_space=pltpu.VMEM)


def params(mib):
    return pltpu.CompilerParams(vmem_limit_bytes=mib * 1024 * 1024)


def cost(flops=0, moved=0):
    return pl.CostEstimate(flops=flops, bytes_accessed=moved, transcendentals=0)


def after(value, *arrays):
    return lax.optimization_barrier((value, *arrays))[0]


def encode(values, used):
    top = jnp.max(jnp.abs(values), axis=1, keepdims=True)
    scale = jnp.maximum(top, 1e-30).astype(jnp.bfloat16).astype(jnp.float32)
    t = values * (GAIN / scale)
    t2 = t * t
    t4 = t2 * t2
    t8 = t4 * t4
    power = t8 * t8
    power = jnp.where(values < 0, -power, power)
    lanes = lax.broadcasted_iota(jnp.int32, values.shape, 1)
    return jnp.where(lanes == used, scale, power).astype(jnp.bfloat16)


def decode(coded, used):
    y = coded.astype(jnp.float32)
    scale = y[:, used : used + 1] * (1.0 / GAIN)
    root = jnp.exp2(jnp.log2(jnp.where(y == 0, 1.0, jnp.abs(y))) * 0.0625) * scale
    value = jnp.where(y == 0, 0.0, jnp.where(y < 0, -root, root))
    lanes = lax.broadcasted_iota(jnp.int32, y.shape, 1)
    return jnp.where(lanes < used, value, 0.0)


def pack_amplitudes(x):
    occ, inner, width, virt = x.shape
    lanes = padded(inner * virt)

    def kernel(x_ref, *out_refs):
        first = 0
        for out_ref, count in zip(out_refs, CHUNKS):
            for i in range(count):
                rows = slice(i * width, (i + 1) * width)
                out_ref[rows, lanes - LANE :] = jnp.zeros((width, LANE), out_ref.dtype)
                for k in range(inner):
                    out_ref[rows, k * virt : (k + 1) * virt] = x_ref[first + i, k]
            first += count

    return pl.pallas_call(
        kernel,
        out_shape=[jax.ShapeDtypeStruct((count * width, lanes), x.dtype) for count in CHUNKS],
        in_specs=[whole()],
        out_specs=[whole() for _ in CHUNKS],
        compiler_params=params(60),
        cost_estimate=cost(moved=4 * x.size),
    )(x)


def pack_integrals(slab, w):
    inner, outer, virt, wide = w.shape
    half = wide // 2
    rows = padded(inner * virt)
    lanes = padded(outer * half)

    def kernel(slab_ref, w_ref, mine_ref, other_ref):
        step = pl.program_id(0)
        low = slab_ref[0] == 0

        @pl.when(step == 0)
        def _():
            for out_ref in (mine_ref, other_ref):
                out_ref[:, lanes - LANE :] = jnp.zeros((rows, LANE), out_ref.dtype)
                out_ref[rows - 16 :, :] = jnp.zeros((16, lanes), out_ref.dtype)

        for k in range(inner):

            @pl.when(step == k)
            def _():
                for j in range(outer):
                    first, second = w_ref[0, j, :, :half], w_ref[0, j, :, half:]
                    at = (slice(k * virt, (k + 1) * virt), slice(j * half, (j + 1) * half))
                    mine_ref[at] = jnp.where(low, first, second)
                    other_ref[at] = jnp.where(low, second, first)

    shape = jax.ShapeDtypeStruct((rows, lanes), w.dtype)
    spec = pl.BlockSpec((rows, lanes), lambda k, s: (0, 0))
    return pl.pallas_call(
        kernel,
        out_shape=[shape, shape],
        grid_spec=pltpu.PrefetchScalarGridSpec(
            num_scalar_prefetch=1,
            grid=(inner,),
            in_specs=[pl.BlockSpec((1, outer, virt, wide), lambda k, s: (k, 0, 0, 0))],
            out_specs=[spec, spec],
        ),
        compiler_params=params(60),
        cost_estimate=cost(moved=8 * w.size),
    )(slab, w)


def multiply(places, gathered, rings, mine, other, used, far):
    depth, lanes = mine.shape
    rows = gathered.shape[-2]

    def kernel(slab_ref, ring_ref, half_ref, g_ref, mine_ref, other_ref, out_ref, *scratch):
        left, right, mine_buf, other_buf, sems = scratch
        half = 1 - half_ref[0] if far else half_ref[0]
        copies = []
        for side, (rows_buf, src, dst) in enumerate(((left, mine_ref, mine_buf), (right, other_ref, other_buf))):
            which = slab_ref[0] if side == 0 else 1 - slab_ref[0]
            if rings:
                block = g_ref.at[:, which, jnp.where(ring_ref[0] == half, 0, 1)]
            else:
                block = g_ref.at[pl.ds(half * RING, RING), which]
            copies.append(
                [
                    pltpu.make_async_copy(block, rows_buf, sems.at[2 * side]),
                    pltpu.make_async_copy(src, dst, sems.at[2 * side + 1]),
                ]
            )
            for copy in copies[-1]:
                copy.start()

        def product(rows_buf, buf):
            return jnp.dot(rows_buf[...].reshape(RING * rows, depth), buf[...], preferred_element_type=jnp.float32)

        for copy in copies[0]:
            copy.wait()
        total = product(left, mine_buf)
        for copy in copies[1]:
            copy.wait()
        total += product(right, other_buf)
        out_ref[...] = (encode(total, used) if far else total).reshape(RING, rows, lanes)

    smem, hbm = pl.BlockSpec(memory_space=pltpu.SMEM), pl.BlockSpec(memory_space=pl.ANY)
    return pl.pallas_call(
        kernel,
        out_shape=jax.ShapeDtypeStruct((RING, rows, lanes), jnp.bfloat16 if far else jnp.float32),
        in_specs=[smem] * 3 + [hbm] * 3,
        out_specs=whole(),
        scratch_shapes=[
            pltpu.VMEM((RING, rows, depth), mine.dtype),
            pltpu.VMEM((RING, rows, depth), mine.dtype),
            pltpu.VMEM(mine.shape, mine.dtype),
            pltpu.VMEM(other.shape, other.dtype),
            pltpu.SemaphoreType.DMA((4,)),
        ],
        compiler_params=params(60),
        cost_estimate=cost(flops=4 * RING * rows * depth * lanes, moved=8 * depth * lanes),
    )(*places, gathered, mine, other)


def add_halves(place, near, far, used):
    _, rows, lanes = near.shape

    def kernel(place_ref, near_ref, far_ref, own_ref, *refs):
        own_ref[...] = near_ref[place_ref[0]] + decode(far_ref[place_ref[0]], used)
        for out_ref, step in zip(refs, STEPS):
            there = (place_ref[0] + step + RING) % RING
            out_ref[...] = encode(near_ref[there] + decode(far_ref[there], used), used)

    shapes = [jax.ShapeDtypeStruct((rows, lanes), jnp.float32)]
    shapes += [jax.ShapeDtypeStruct((rows, lanes), jnp.bfloat16)] * len(STEPS)
    return pl.pallas_call(
        kernel,
        out_shape=shapes,
        in_specs=[pl.BlockSpec(memory_space=pltpu.SMEM), whole(), whole()],
        out_specs=[whole() for _ in shapes],
        compiler_params=params(60),
        cost_estimate=cost(moved=32 * rows * lanes),
    )(place, near, far)


def add_up(parts, used):
    rows, lanes = parts[0].shape[-2:]

    def kernel(*refs):
        sum_ref, coded_ref = refs[-2:]
        total = 0.0
        for ref in refs[:-2]:
            if len(ref.shape) == 3:
                for n in range(ref.shape[0]):
                    total += decode(ref[n], used)
            elif ref.dtype == jnp.float32:
                total += ref[...]
            else:
                total += decode(ref[...], used)
        sum_ref[...] = total
        coded_ref[...] = encode(total, used)

    return pl.pallas_call(
        kernel,
        out_shape=[
            jax.ShapeDtypeStruct((rows, lanes), jnp.float32),
            jax.ShapeDtypeStruct((rows, lanes), jnp.bfloat16),
        ],
        in_specs=[whole() for _ in parts],
        out_specs=[whole(), whole()],
        compiler_params=params(60),
        cost_estimate=cost(moved=64 * rows * lanes),
    )(*parts)


def subtract(sums, mirrored, chunk, residual, width, occ, virt):
    used = occ * virt
    count = len(sums)
    first = sum(CHUNKS[:chunk])
    columns = range(first, first + CHUNKS[chunk])

    def kernel(*refs):
        sum_refs, mirror_ref = refs[:count], refs[count]
        out_ref, flat, part, sem = refs[-4:]
        flat[...] = decode(mirror_ref[...], used)
        at = 0
        for ref, n in zip(sum_refs, CHUNKS):
            for i in range(n):
                for j in columns:
                    here = ref[i * width : (i + 1) * width, j * virt : (j + 1) * virt]
                    there = slice((j - first) * width, (j - first + 1) * width)
                    part[at, j - first] = here - flat[there, at * virt : (at + 1) * virt]
                at += 1
        copy = pltpu.make_async_copy(part, out_ref.at[:, first : first + len(columns)], sem)
        copy.start()
        copy.wait()

    hbm = pl.BlockSpec(memory_space=pl.ANY)
    before = [] if residual is None else [residual]
    return pl.pallas_call(
        kernel,
        out_shape=jax.ShapeDtypeStruct((occ, occ, width, virt), jnp.float32),
        in_specs=[whole() for _ in range(count + 1)] + [hbm] * len(before),
        out_specs=hbm,
        scratch_shapes=[
            pltpu.VMEM(mirrored.shape, jnp.float32),
            pltpu.VMEM((occ, len(columns), width, virt), jnp.float32),
            pltpu.SemaphoreType.DMA(()),
        ],
        input_output_aliases={count + 1: 0} if before else {},
        compiler_params=params(60),
        cost_estimate=cost(moved=16 * occ * len(columns) * width * virt),
    )(*sums, mirrored, *before)


def on_device(amplitudes, integrals):
    occ, width, _, _ = amplitudes.shape
    out_occ = integrals.shape[2]
    out_virt = integrals.shape[3] // lax.axis_size("slab")
    used = out_occ * out_virt
    rows, cols = lax.axis_size("row"), lax.axis_size("col")
    slab = lax.axis_index("slab").astype(jnp.int32).reshape(1)
    mirror_pairs = [(r * cols + c, c * cols + r) for r in range(rows) for c in range(cols)]
    row = lax.axis_index("row").astype(jnp.int32)
    half, place = (row // RING).reshape(1), (row % RING).reshape(1)
    ring = (lax.axis_index("col") // RING).astype(jnp.int32).reshape(1)
    swap = [(0, 1), (1, 0)]
    cross = [(c, (c + RING) % cols) for c in range(cols)]
    groups = [list(range(n, n + 2 * RING)) for n in range(0, 2 * cols, 2 * RING)]

    packed, rest = pack_amplitudes(jnp.transpose(amplitudes, (0, 2, 1, 3)))
    early = lax.all_gather(packed, ("col", "slab"), axis=0)
    early = early.reshape(cols, 2, *packed.shape)
    across = lax.ppermute(rest, "col", cross)
    mine, sent = pack_integrals(after(slab, across), jnp.transpose(integrals, (0, 2, 1, 3)))
    other = lax.ppermute(sent, "slab", swap)
    pair = jnp.stack([rest, across])
    late = lax.all_gather(after(pair, early, other), ("col", "slab"), axis=0, axis_index_groups=groups)
    late = late.reshape(RING, 2, *pair.shape)

    def shifted(value, step):
        pairs = [(r, r // RING * RING + (r + step) % RING) for r in range(rows)]
        return lax.ppermute(value, "row", pairs)

    def mirror(parts):
        total, again = add_up(parts, used)
        return total, lax.ppermute(again, ("row", "col"), mirror_pairs)

    def product(token, source, rings, far):
        return multiply((after(slab, *token), ring, half), source, rings, mine, other, used, far)

    def around(near, far):
        own, *others = add_halves(place, near, far, used)
        return [own, *(shifted(part, step) for part, step in zip(others, STEPS))]

    far = product((), early, False, True)
    early_far = lax.ppermute(far, "row", cross)
    early_near = product((far,), early, False, False)
    far = product((early_near,), late, True, True)
    late_far = lax.ppermute(far, "row", cross)
    early_parts = around(early_near, early_far)
    late_near = product((far, early_parts[0]), late, True, False)
    late_parts = around(late_near, late_far)
    first, again = add_up(early_parts, used)
    second, last = add_up(late_parts, used)
    again = after(again, *late_parts)
    sums = (first, second)
    mirrored = [lax.ppermute(part, ("row", "col"), mirror_pairs) for part in (again, last)]
    residual = None
    for chunk, block in enumerate(mirrored):
        residual = subtract(sums, block, chunk, residual, width, occ, out_virt)
    return jnp.transpose(residual, (0, 2, 1, 3))


def solution(mesh):
    return jax.shard_map(
        on_device,
        mesh=mesh,
        in_specs=(P("col", None, "row", "slab"), P("row", "slab", "col", None)),
        out_specs=P("row", None, "col", "slab"),
        check_vma=False,
    )
```
